32 devices in a mesh: half: 2 (over y), shard: 16 (over z, x, core).
Axes of the slice: x: 2, y: 2, z: 4, core: 2. Of those that a mesh axis runs over, the one named last changes fastest.
Arguments:
- recording: float32 [32, 2048, 1024], P('half', 'shard'), may hold values from -600 to 600
- source_channels: int32 [256], replicated, may hold values from 0 to 2047, as said below
Outputs:
- correlations: float32 [256, 2048, 512], P('half', 'shard')
The draws below stay inside these ranges and needn't reach their ends.
Inputs may be any that keep to these rules, and one draw needn't show every extreme that they name: `source_channels`: distinct channel indices.
All inputs are finite; a program needn't handle non-finite values.
Results may differ from the reference program's by a relative error of at most 0.000071.
Values sent between devices are 32-bit elements; how exact they have to be, the bound alone decides.
No kernel may reach another device: no remote copies, remote signals or barrier semaphores. Data moves between devices by JAX's collectives and lax.ppermute only.
A program may use at most 128 MiB of HBM per device.

```python
import jax
import jax.numpy as jnp
from jax import lax

C = 2048
L = 1024
F = 128
LAGS = 512
SMOOTH = 2
NSRC = 256
SEG = 32


def draw_recording(key, part):
    base = jax.random.fold_in(key, 11)
    key_chan, key_seg, key_noise = jax.random.split(base, 3)
    chan_gain = jnp.exp(jax.random.uniform(key_chan, (1, C, 1), jnp.float32) * jnp.log(10.0))
    seg_gain = jnp.exp(jax.random.uniform(key_seg, (SEG, 1, 1), jnp.float32) * jnp.log(10.0))
    signal = jnp.clip(jax.random.normal(key_noise, (SEG, C, L), jnp.float32), -6.0, 6.0)
    return (signal * chan_gain * seg_gain).astype(jnp.float32)


def draw_source_channels(key, part):
    base = jax.random.fold_in(key, 23)
    key_pick, key_order = jax.random.split(base, 2)
    inner = jax.random.permutation(key_pick, C - 2)[:NSRC - 2] + 1
    chosen = jnp.concatenate((inner.astype(jnp.int32), jnp.array([0, C - 1], dtype=jnp.int32)))
    order = jax.random.permutation(key_order, NSRC)
    return chosen[order].astype(jnp.int32)


def setup_inputs(seed: int = 0) -> dict:
    streams_of = jax.random.split(jax.random.key(seed), 3)
    recording = draw_recording(jax.random.fold_in(streams_of[2], 71), 0)
    source_channels = draw_source_channels(jax.random.fold_in(streams_of[2], 71), 0)
    return {"recording": recording, "source_channels": source_channels}


water_level = 0.2
epsilon = 1e-05

def forward_table(samples, freq_count):
    bins = jnp.arange(freq_count, dtype=jnp.int32) + 1
    times = jnp.arange(samples, dtype=jnp.int32)
    phase = bins[:, None] * times[None, :] % samples
    angle = 2.0 * jnp.pi * phase.astype(jnp.float32) / samples
    taper = 0.5 - 0.5 * jnp.cos(2.0 * jnp.pi * times.astype(jnp.float32) / samples)
    return jnp.stack((jnp.cos(angle) * taper[None, :], -jnp.sin(angle) * taper[None, :]), axis=1)

def inverse_table(samples, freq_count, lag_count, segments):
    bins = jnp.arange(freq_count, dtype=jnp.int32) + 1
    shifts = jnp.arange(lag_count, dtype=jnp.int32) - lag_count // 2
    phase = bins[:, None] * shifts[None, :] % samples
    angle = 2.0 * jnp.pi * phase.astype(jnp.float32) / samples
    scale = 1.0 / jnp.sqrt(jnp.float32(segments * freq_count))
    return jnp.stack((jnp.cos(angle) * scale, -jnp.sin(angle) * scale), axis=1)

def whiten(spectra):
    magnitude = jnp.sqrt(spectra[:, 0] * spectra[:, 0] + spectra[:, 1] * spectra[:, 1])
    freq_count = magnitude.shape[0]
    padded = jnp.pad(magnitude, ((SMOOTH, SMOOTH), (0, 0), (0, 0)))
    smoothed = padded[0:freq_count]
    for offset in range(1, 2 * SMOOTH + 1):
        smoothed = smoothed + padded[offset:offset + freq_count]
    smoothed = smoothed / (2 * SMOOTH + 1)
    water_mark = lax.optimization_barrier(jnp.mean(magnitude, axis=0, keepdims=True))
    divisor = smoothed + water_level * water_mark + epsilon
    return spectra / divisor[:, None]

def correlate(whitened, indices):
    sources = jnp.take(whitened, indices, axis=2)
    src_real, src_imag = (sources[:, 0], sources[:, 1])
    rec_real, rec_imag = (whitened[:, 0], whitened[:, 1])
    high = lax.Precision.HIGHEST
    cross_real = jnp.einsum('fnx,fcx->fnc', src_real, rec_real, precision=high) + jnp.einsum('fnx,fcx->fnc', src_imag, rec_imag, precision=high)
    cross_imag = jnp.einsum('fnx,fcx->fnc', src_real, rec_imag, precision=high) - jnp.einsum('fnx,fcx->fnc', src_imag, rec_real, precision=high)
    return jnp.stack((cross_real, cross_imag), axis=1)

def reference(recording, source_channels):
    forward = forward_table(L, F)
    spectra = jnp.einsum('fqt,sct->fqcs', forward, recording, precision=lax.Precision.HIGHEST)
    whitened = whiten(spectra)
    cross = correlate(whitened, source_channels)
    backward = inverse_table(L, F, LAGS, SEG)
    return jnp.einsum('fqnc,fql->ncl', cross, backward, precision=lax.Precision.HIGHEST)
```

```python
import functools

import jax
import jax.numpy as jnp
import numpy as np
from jax import lax
from jax.experimental import pallas as pl
from jax.experimental.pallas import tpu as pltpu
from jax.sharding import PartitionSpec as P

F = 128
LAGS = 512
SMOOTH = 2
SEG = 32
CHUNKS = 4

water_level = 0.2
epsilon = 1e-05

BF16 = jnp.bfloat16
F32 = jnp.float32


def forward_table(samples):
    bins = np.arange(F, dtype=np.int64) + 1
    times = np.arange(samples, dtype=np.int64)
    angle = 2.0 * np.pi * (bins[:, None] * times[None, :] % samples) / samples
    taper = 0.5 - 0.5 * np.cos(2.0 * np.pi * times / samples)
    return np.concatenate((np.cos(angle) * taper, -np.sin(angle) * taper)).astype(np.float32)


def inverse_table(samples):
    bins = np.arange(F, dtype=np.int64) + 1
    shifts = np.arange(LAGS, dtype=np.int64) - LAGS // 2
    angle = 2.0 * np.pi * (bins[:, None] * shifts[None, :] % samples) / samples
    scale = 1.0 / np.sqrt(float(SEG * F))
    return np.concatenate((np.cos(angle) * scale, -np.sin(angle) * scale)).astype(np.float32)


def split_const(table):
    high = table.astype(jnp.bfloat16)
    low = (table - high.astype(np.float32)).astype(jnp.bfloat16)
    return high, low


def split(x):
    high = x.astype(BF16)
    low = (x - high.astype(F32)).astype(BF16)
    return high, low


def dot_nt(a, b):
    return lax.dot_general(a, b, (((1,), (1,)), ((), ())), preferred_element_type=F32)


def dot_nn(a, b):
    return lax.dot_general(a, b, (((1,), (0,)), ((), ())), preferred_element_type=F32)


def whiten_tile(real, imag):
    magnitude = jnp.sqrt(real * real + imag * imag)
    row = lax.broadcasted_iota(jnp.int32, magnitude.shape, 0)
    smoothed = magnitude
    for offset in range(1, SMOOTH + 1):
        smoothed = smoothed + jnp.where(row >= offset, pltpu.roll(magnitude, offset, 0), 0.0)
        smoothed = smoothed + jnp.where(row < F - offset, pltpu.roll(magnitude, F - offset, 0), 0.0)
    water_mark = jnp.mean(magnitude, axis=0, keepdims=True)
    divisor = smoothed * (1.0 / (2 * SMOOTH + 1)) + water_level * water_mark + epsilon
    return real / divisor, imag / divisor


def spectra_kernel(place_ref, rec_ref, hi_ref, lo_ref, idx_ref, white_ref, *sent, segs, shards):
    step = pl.program_id(0)
    per, channels, samples = rec_ref.shape
    high, low = split(rec_ref[...].reshape(per * channels, samples))
    spectra = dot_nt(hi_ref[...], high) + (dot_nt(lo_ref[...], high) + dot_nt(hi_ref[...], low))
    for i in range(per):
        lanes = slice(i * channels, (i + 1) * channels)
        real, imag = whiten_tile(spectra[:F, lanes], spectra[F:, lanes])
        seg = step * per + i
        white_ref[pl.ds(seg, F, stride=2 * segs), :] = real
        white_ref[pl.ds(seg + segs, F, stride=2 * segs), :] = imag

    @pl.when(step == pl.num_programs(0) - 1)
    def _():
        shard, half = place_ref[0], place_ref[1]
        nsrc = idx_ref.shape[0]
        per_half = nsrc // 2
        size = per_half // CHUNKS
        rows = F // shards * 2 * segs
        own = pl.multiple_of(half * per_half, per_half)
        other = pl.multiple_of((1 - half) * per_half, per_half)
        index = jnp.concatenate((idx_ref[pl.ds(own, per_half), :], idx_ref[pl.ds(other, per_half), :]))
        lane = lax.broadcasted_iota(jnp.int32, (nsrc, channels), 1)
        hot = (index - shard * channels == lane).astype(F32).astype(BF16)
        hot = jnp.concatenate((hot, hot), axis=1)
        for r in range(shards):
            start = pl.multiple_of((shard ^ r) * rows, rows)
            high, low = split(white_ref[pl.ds(start, rows), :])
            got = dot_nt(hot, jnp.concatenate((high, low), axis=1))
            for j in range(CHUNKS):
                for h in range(2):
                    at = h * per_half + j * size
                    where, slot = place_of(r)
                    sent[4 * j + where][slot, h] = got[at : at + size]


def place_of(r):
    return (r & 1) * 2 + (r >> 1 & 1), r >> 2


def forward(recording, source_channels, shard, half, shards):
    segs, channels, samples = recording.shape
    per = 2
    nsrc = source_channels.shape[0]
    size = nsrc // 2 // CHUNKS
    lanes = F // shards * 2 * segs
    high, low = split_const(forward_table(samples))
    full = lambda shape: pl.BlockSpec(shape, lambda s, p: (0,) * len(shape))
    block = (shards // 4, 2, size, lanes)
    outs = pl.pallas_call(
        functools.partial(spectra_kernel, segs=segs, shards=shards),
        grid_spec=pltpu.PrefetchScalarGridSpec(
            num_scalar_prefetch=1,
            grid=(segs // per,),
            in_specs=[
                pl.BlockSpec((per, channels, samples), lambda s, p: (s, 0, 0)),
                full((2 * F, samples)),
                full((2 * F, samples)),
                full((nsrc, 1)),
            ],
            out_specs=[full((F * 2 * segs, channels))] + [full(block)] * (4 * CHUNKS),
        ),
        out_shape=[jax.ShapeDtypeStruct((F * 2 * segs, channels), F32)]
        + [jax.ShapeDtypeStruct(block, F32)] * (4 * CHUNKS),
        compiler_params=pltpu.CompilerParams(vmem_limit_bytes=40 * 2**20, dimension_semantics=("arbitrary",)),
        cost_estimate=pl.CostEstimate(flops=6 * 10**9, bytes_accessed=16 * 2**20, transcendentals=0),
        name="forward_whiten",
    )(jnp.stack((shard, half)), recording, high, low, source_channels[:, None])
    return outs[0], [outs[1 + 4 * j : 5 + 4 * j] for j in range(CHUNKS)]


def stack_kernel(place_ref, own_ref, oth_ref, hi_ref, lo_ref, *refs, shards, segs, size, per, aliased):
    blocks = refs[: 2 * shards]
    out_ref, real_ref, imag_ref, src_ref = refs[2 * shards + aliased :]
    step = pl.program_id(0)
    channels = own_ref.shape[1]
    bins = F // shards
    width = 2 * segs

    @pl.when(step == 0)
    def _():
        for r in range(shards):
            src_ref[r, 0] = blocks[2 * r][...]
            src_ref[r, 1] = blocks[2 * r + 1][...]

        def block(r, carry):
            base = (place_ref[0] ^ r) * bins
            own_all = src_ref[r, 0]
            oth_all = src_ref[r, 1]
            for i in range(bins):
                at = pl.multiple_of((base + i) * width, width)
                w = jnp.concatenate((own_ref[pl.ds(at, width), :], oth_ref[pl.ds(at, width), :]))
                high, low = split(w)
                turn = lambda v: jnp.concatenate(
                    (v[segs : 2 * segs], -v[:segs], v[3 * segs :], -v[2 * segs : 3 * segs])
                )
                rhs = jnp.concatenate(
                    (
                        jnp.concatenate((high, high, low)),
                        jnp.concatenate((turn(high), turn(high), turn(low))),
                    ),
                    axis=1,
                )
                lanes = slice(i * width, (i + 1) * width)
                shigh, slow = split(jnp.concatenate((own_all[:, lanes], oth_all[:, lanes]), axis=1))
                lhs = jnp.concatenate((shigh, slow, shigh), axis=1)
                row = pl.multiple_of((base + i) * size, size)
                cross = dot_nn(lhs, rhs)
                real_ref[pl.ds(row, size), :] = cross[:, :channels]
                imag_ref[pl.ds(row, size), :] = cross[:, channels:]
            return carry

        lax.fori_loop(0, shards, block, 0)

    for i in range(per):
        n = step * per + i
        both = [jnp.transpose(ref[pl.ds(n, F, stride=size), :]) for ref in (real_ref, imag_ref)]
        high, low = split(jnp.concatenate(both, axis=1))
        out_ref[i] = dot_nn(high, hi_ref[...]) + (dot_nn(low, hi_ref[...]) + dot_nn(high, lo_ref[...]))


def correlate(j, previous, shard, own, other, blocks, shards, segs, samples, nsrc):
    per_half = nsrc // 2
    size = per_half // CHUNKS
    per = 4
    channels = own.shape[1]
    high, low = split_const(inverse_table(samples))
    full = lambda shape: pl.BlockSpec(shape, lambda s, p: (0,) * len(shape))
    steps = size // per
    aliased = previous is not None
    operands = [own, other, high, low, *blocks]
    in_specs = [full(x.shape) for x in operands]
    if aliased:
        operands.append(previous)
        in_specs.append(pl.BlockSpec(memory_space=pl.ANY))
    return pl.pallas_call(
        functools.partial(stack_kernel, shards=shards, segs=segs, size=size, per=per, aliased=aliased),
        grid_spec=pltpu.PrefetchScalarGridSpec(
            num_scalar_prefetch=1,
            grid=(steps,),
            in_specs=in_specs,
            out_specs=pl.BlockSpec((per, channels, LAGS), lambda s, p: (j * steps + s, 0, 0)),
            scratch_shapes=[
                pltpu.VMEM((F * size, channels), F32),
                pltpu.VMEM((F * size, channels), F32),
                pltpu.VMEM((shards, 2, size, F // shards * 2 * segs), F32),
            ],
        ),
        out_shape=jax.ShapeDtypeStruct((per_half, channels, LAGS), F32),
        input_output_aliases={len(operands): 0} if aliased else {},
        compiler_params=pltpu.CompilerParams(vmem_limit_bytes=48 * 2**20, dimension_semantics=("arbitrary",)),
        cost_estimate=pl.CostEstimate(flops=5 * 10**9, bytes_accessed=16 * 2**20, transcendentals=0),
        name="stack_lags",
    )(shard[None], *operands)


def swap(x, axis, bits):
    return lax.ppermute(x, axis, [(i, i ^ bits) for i in range(lax.axis_size(axis))])


def spread_sources(parts):
    even, even_x, odd, odd_x = parts
    shards = 4 * even.shape[0]
    even, even_x = even + swap(odd, "shard", 1), even_x + swap(odd_x, "shard", 1)
    even = even + swap(even_x, "shard", 2)
    mine = even[0]
    for k in range(1, shards // 4):
        mine = mine + swap(even[k], "shard", 4 * k)
    pair = [mine[0], swap(mine[1], "half", 1)]
    blocks = {}
    for h in range(2):
        for k in range(shards // 4):
            blocks[4 * k, h] = swap(pair[h], "shard", 4 * k) if k else pair[h]
    for bit in (2, 1):
        for (r, h), x in list(blocks.items()):
            blocks[r ^ bit, h] = swap(x, "shard", bit)
    return [blocks[r, h] for r in range(shards) for h in range(2)]


def body(recording, source_channels):
    segs, _, samples = recording.shape
    shards = lax.axis_size("shard")
    shard, half = lax.axis_index("shard"), lax.axis_index("half")
    own, parts = forward(recording, source_channels, shard, half, shards)
    other = swap(own, "half", 1)
    result = None
    for j in range(CHUNKS):
        blocks = spread_sources(parts[j])
        result = correlate(
            j, result, shard, own, other, blocks, shards, segs, samples, source_channels.shape[0]
        )
    return result


def plain_forward_table(samples, freq_count):
    table = forward_table(samples)
    return jnp.stack((table[:freq_count], table[freq_count:]), axis=1)


def plain_inverse_table(samples, freq_count):
    table = inverse_table(samples)
    return jnp.stack((table[:freq_count], table[freq_count:]), axis=1)


def plain_whiten(spectra):
    magnitude = jnp.sqrt(spectra[:, 0] * spectra[:, 0] + spectra[:, 1] * spectra[:, 1])
    freq_count = magnitude.shape[0]
    padded = jnp.pad(magnitude, ((SMOOTH, SMOOTH), (0, 0), (0, 0)))
    smoothed = padded[0:freq_count]
    for offset in range(1, 2 * SMOOTH + 1):
        smoothed = smoothed + padded[offset : offset + freq_count]
    smoothed = smoothed / (2 * SMOOTH + 1)
    water_mark = jnp.mean(magnitude, axis=0, keepdims=True)
    divisor = smoothed + water_level * water_mark + epsilon
    return spectra / divisor[:, None]


def plain_correlate(whitened, indices):
    sources = jnp.take(whitened, indices, axis=2)
    src_real, src_imag = (sources[:, 0], sources[:, 1])
    rec_real, rec_imag = (whitened[:, 0], whitened[:, 1])
    high = lax.Precision.HIGHEST
    cross_real = jnp.einsum("fnx,fcx->fnc", src_real, rec_real, precision=high) + jnp.einsum(
        "fnx,fcx->fnc", src_imag, rec_imag, precision=high
    )
    cross_imag = jnp.einsum("fnx,fcx->fnc", src_real, rec_imag, precision=high) - jnp.einsum(
        "fnx,fcx->fnc", src_imag, rec_real, precision=high
    )
    return jnp.stack((cross_real, cross_imag), axis=1)


def plain_body(recording, source_channels):
    samples = recording.shape[2]
    high = lax.Precision.HIGHEST
    spectra = jnp.einsum("fqt,sct->fqcs", plain_forward_table(samples, F), recording, precision=high)
    whitened = plain_whiten(spectra)
    by_freq = lax.all_to_all(whitened, "shard", split_axis=0, concat_axis=2, tiled=True)
    per_half = source_channels.shape[0] // lax.axis_size("half")
    own_sources = lax.dynamic_slice_in_dim(source_channels, lax.axis_index("half") * per_half, per_half)
    combined = jnp.concatenate((by_freq, swap(by_freq, "half", 1)), axis=3)
    cross = plain_correlate(combined, own_sources)
    cross = lax.all_to_all(cross, "shard", split_axis=3, concat_axis=0, tiled=True)
    return jnp.einsum("fqnc,fql->ncl", cross, plain_inverse_table(samples, F), precision=high)


def solution(mesh):
    def run(recording, source_channels):
        shards = lax.axis_size("shard")
        fits = recording.shape[1] % 128 == 0 and shards % 4 == 0 and F % shards == 0
        return (body if fits else plain_body)(recording, source_channels)

    return jax.shard_map(
        run,
        mesh=mesh,
        in_specs=(P("half", "shard", None), P()),
        out_specs=P("half", "shard", None),
        check_vma=False,
    )
```

```python
import functools

import jax
import jax.numpy as jnp
import numpy as np
from jax import lax
from jax.experimental import pallas as pl
from jax.experimental.pallas import tpu as pltpu
from jax.sharding import PartitionSpec as P

F = 128
LAGS = 512
SMOOTH = 2
SEG = 32
CHUNKS = 1
CAP = 32

water_level = 0.2
epsilon = 1e-05

BF16 = jnp.bfloat16
F32 = jnp.float32


def forward_table(samples):
    bins = np.arange(F, dtype=np.int64) + 1
    times = np.arange(samples, dtype=np.int64)
    angle = 2.0 * np.pi * (bins[:, None] * times[None, :] % samples) / samples
    taper = 0.5 - 0.5 * np.cos(2.0 * np.pi * times / samples)
    return np.concatenate((np.cos(angle) * taper, -np.sin(angle) * taper)).astype(np.float32)


def inverse_table(samples):
    bins = np.arange(F, dtype=np.int64) + 1
    shifts = np.arange(LAGS, dtype=np.int64) - LAGS // 2
    angle = 2.0 * np.pi * (bins[:, None] * shifts[None, :] % samples) / samples
    scale = 1.0 / np.sqrt(float(SEG * F))
    return np.concatenate((np.cos(angle) * scale, -np.sin(angle) * scale)).astype(np.float32)


def split_const(table):
    high = table.astype(jnp.bfloat16)
    low = (table - high.astype(np.float32)).astype(jnp.bfloat16)
    return high, low


def split(x):
    high = x.astype(BF16)
    low = (x - high.astype(F32)).astype(BF16)
    return high, low


def dot_nt(a, b):
    return lax.dot_general(a, b, (((1,), (1,)), ((), ())), preferred_element_type=F32)


def dot_nn(a, b):
    return lax.dot_general(a, b, (((1,), (0,)), ((), ())), preferred_element_type=F32)


def whiten_tile(real, imag):
    magnitude = jnp.sqrt(real * real + imag * imag)
    row = lax.broadcasted_iota(jnp.int32, magnitude.shape, 0)
    smoothed = magnitude
    for offset in range(1, SMOOTH + 1):
        smoothed = smoothed + jnp.where(row >= offset, pltpu.roll(magnitude, offset, 0), 0.0)
        smoothed = smoothed + jnp.where(row < F - offset, pltpu.roll(magnitude, F - offset, 0), 0.0)
    water_mark = jnp.mean(magnitude, axis=0, keepdims=True)
    divisor = smoothed * (1.0 / (2 * SMOOTH + 1)) + water_level * water_mark + epsilon
    return real / divisor, imag / divisor


def as_column(row):
    n = row.shape[1]
    here = lax.broadcasted_iota(jnp.int32, (n, n), 0) == lax.broadcasted_iota(jnp.int32, (n, n), 1)
    return jnp.sum(jnp.where(here, row.astype(F32), 0.0), axis=1, keepdims=True).astype(jnp.int32)


def ranks(col, row, channels, axis):
    same = col // channels == row // channels
    first = lax.broadcasted_iota(jnp.int32, same.shape, axis) < lax.broadcasted_iota(jnp.int32, same.shape, 1 - axis)
    return jnp.sum(jnp.where(same & first, 1.0, 0.0), axis=axis, keepdims=True).astype(jnp.int32)


def spectra_kernel(place_ref, rec_ref, hi_ref, lo_ref, row_ref, first_ref, second_ref, held_ref, *, segs):
    step = pl.program_id(0)
    per, channels, samples = rec_ref.shape
    high, low = split(rec_ref[...].reshape(per * channels, samples))
    spectra = dot_nt(hi_ref[...], high) + (dot_nt(lo_ref[...], high) + dot_nt(hi_ref[...], low))
    for i in range(per):
        lanes = slice(i * channels, (i + 1) * channels)
        real, imag = whiten_tile(spectra[:F, lanes], spectra[F:, lanes])
        seg = step * per + i
        for ref, start in ((first_ref, 0), (second_ref, first_ref.shape[0] // (2 * segs))):
            count = ref.shape[0] // (2 * segs)
            ref[pl.ds(seg, count, stride=2 * segs), :] = real[start : start + count]
            ref[pl.ds(seg + segs, count, stride=2 * segs), :] = imag[start : start + count]

    @pl.when(step == pl.num_programs(0) - 1)
    def _():
        shards, cap, rows = held_ref.shape
        shard = place_ref[0]
        row = row_ref[...]
        col = as_column(row)
        nsrc = col.shape[0]
        rank = jnp.where(row // channels == shard, ranks(col, row, channels, 0), -1)
        chosen = (lax.broadcasted_iota(jnp.int32, (cap, nsrc), 0) == rank).astype(F32).astype(BF16)
        lane = lax.broadcasted_iota(jnp.int32, (nsrc, channels), 1)
        where = (col - shard * channels == lane).astype(F32).astype(BF16)
        hot = dot_nn(chosen, where).astype(BF16)
        hot = jnp.concatenate((hot, hot), axis=1)
        for d in range(shards):
            cut = first_ref.shape[0] // rows
            ref, at = (first_ref, d) if d < cut else (second_ref, d - cut)
            high, low = split(ref[at * rows : (at + 1) * rows, :])
            held_ref[d] = dot_nt(hot, jnp.concatenate((high, low), axis=1))


def whole(shape):
    return pl.BlockSpec(shape, lambda *_: (0,) * len(shape))


def first_blocks(shards):
    return 3 * shards // 8


def forward(recording, row, shard, shards):
    segs, channels, samples = recording.shape
    per = 4
    nsrc = row.shape[1]
    rows = F // shards * 2 * segs
    held = (shards, CAP, rows)
    cut = first_blocks(shards)
    white = [(cut * rows, channels), ((shards - cut) * rows, channels)]
    high, low = split_const(forward_table(samples))
    return pl.pallas_call(
        functools.partial(spectra_kernel, segs=segs),
        grid_spec=pltpu.PrefetchScalarGridSpec(
            num_scalar_prefetch=1,
            grid=(segs // per,),
            in_specs=[
                pl.BlockSpec((per, channels, samples), lambda s, p: (s, 0, 0)),
                whole((2 * F, samples)),
                whole((2 * F, samples)),
                whole((1, nsrc)),
            ],
            out_specs=[whole(x) for x in (*white, held)],
        ),
        out_shape=[jax.ShapeDtypeStruct(x, F32) for x in (*white, held)],
        compiler_params=pltpu.CompilerParams(vmem_limit_bytes=60 * 2**20, dimension_semantics=("arbitrary",)),
        cost_estimate=pl.CostEstimate(flops=6 * 10**9, bytes_accessed=16 * 2**20, transcendentals=0),
        name="forward_whiten",
    )(shard[None], recording, high, low, row)


def order_kernel(place_ref, got_ref, row_ref, *outs, channels):
    row = row_ref[...]
    col = as_column(row)
    nsrc = col.shape[0]
    entries = got_ref.shape[0]
    at = col // channels * CAP + ranks(col, row, channels, 1)
    hot = (at == lax.broadcasted_iota(jnp.int32, (nsrc, entries), 1)).astype(F32).astype(BF16)
    high, low = split(got_ref[...])
    rows = dot_nn(hot, high) + dot_nn(hot, low)
    size = outs[0].shape[0]
    per_half = nsrc // 2
    for h in range(2):

        @pl.when(place_ref[1] == h)
        def _():
            for k, out in enumerate(outs):
                start = ((k // CHUNKS) ^ h) * per_half + k % CHUNKS * size
                out[...] = rows[start : start + size]


def in_order(got, row, shard, half, channels):
    nsrc = row.shape[1]
    size = nsrc // 2 // CHUNKS
    shape = (size, got.shape[1])
    return pl.pallas_call(
        functools.partial(order_kernel, channels=channels),
        grid_spec=pltpu.PrefetchScalarGridSpec(
            num_scalar_prefetch=1,
            grid=(1,),
            in_specs=[whole(got.shape), whole((1, nsrc))],
            out_specs=[whole(shape)] * (2 * CHUNKS),
        ),
        out_shape=[jax.ShapeDtypeStruct(shape, F32)] * (2 * CHUNKS),
        compiler_params=pltpu.CompilerParams(vmem_limit_bytes=16 * 2**20),
        cost_estimate=pl.CostEstimate(flops=10**8, bytes_accessed=2**20, transcendentals=0),
        name="order_sources",
    )(jnp.stack((shard, half)), got, row)


def any_order(white, source_channels, half, shards):
    channels = white.shape[1]
    bins = white.reshape(shards, -1, channels)
    bins = lax.all_to_all(bins, "shard", split_axis=0, concat_axis=2, tiled=True)[0]
    rows = jnp.take(bins, source_channels, axis=1).T
    per_half = rows.shape[0] // 2
    mine = lax.dynamic_slice_in_dim(rows, half * per_half, per_half)
    others = lax.dynamic_slice_in_dim(rows, (1 - half) * per_half, per_half)
    return [*jnp.split(mine, CHUNKS), *jnp.split(others, CHUNKS)]


def pair_kernel(own_ref, oth_ref, out_ref, *, width):
    own, oth = own_ref[...], oth_ref[...]
    parts = []
    for i in range(own.shape[1] // width):
        lanes = slice(i * width, (i + 1) * width)
        parts += [own[:, lanes], oth[:, lanes]]
    out_ref[...] = jnp.concatenate(parts, axis=1)


def pair_halves(own, other, width):
    size, lanes = own.shape
    return pl.pallas_call(
        functools.partial(pair_kernel, width=width),
        out_shape=jax.ShapeDtypeStruct((size, 2 * lanes), F32),
        cost_estimate=pl.CostEstimate(flops=10**6, bytes_accessed=2**20, transcendentals=0),
        name="pair_halves",
    )(own, other)


def stack_kernel(place_ref, own0_ref, own1_ref, oth0_ref, oth1_ref, hi_ref, lo_ref, *refs, shards, pitch):
    blocks = refs[:shards]
    out_ref, real_ref, imag_ref, src_ref = refs[-4:]
    step = pl.program_id(0)
    per, channels, lags = out_ref.shape
    size, lanes = blocks[0].shape
    bins = F // shards
    width = lanes // bins // 2
    segs = width // 2
    cut = own0_ref.shape[0] // (bins * width)

    def turn(v):
        return jnp.concatenate((v[segs : 2 * segs], -v[:segs], v[3 * segs :], -v[2 * segs : 3 * segs]))

    def block(owner, own_ref, oth_ref, skip):
        zero = jnp.zeros((2 * width, channels), BF16)
        for two in range(0, bins, 2):
            shigh, slow = split(src_ref[place_ref[0] ^ owner, :, two * 2 * width : (two + 2) * 2 * width])
            for i in range(two, two + 2):
                rows = pl.ds(pl.multiple_of(((owner - skip) * bins + i) * width, width), width)
                high, low = split(jnp.concatenate((own_ref[rows, :], oth_ref[rows, :])))
                order = lambda h, l: jnp.concatenate((h, h, l, zero) if i == two else (h, h, zero, l))
                rhs = jnp.concatenate((order(high, low), order(turn(high), turn(low))), axis=1)
                at = slice((i - two) * 2 * width, (i - two + 1) * 2 * width)
                cross = dot_nn(jnp.concatenate((shigh[:, at], slow[:, at], shigh), axis=1), rhs)
                to = pl.ds(pl.multiple_of((owner * bins + i) * pitch, 8), size)
                real_ref[to, :] = cross[:, :channels]
                imag_ref[to, :] = cross[:, channels:]

    @pl.when(step == 0)
    def _():
        for r in range(shards):
            src_ref[r] = blocks[r][...]

        def first(owner, carry):
            block(owner, own0_ref, oth0_ref, 0)
            return carry

        def second(owner, carry):
            block(owner, own1_ref, oth1_ref, cut)
            return carry

        lax.fori_loop(0, cut, first, 0, unroll=2)
        lax.fori_loop(cut, shards, second, 0, unroll=2)

    table = jnp.concatenate((hi_ref[...], hi_ref[...], lo_ref[...]))
    rows = []
    for i in range(per):
        n = step * per + i
        both = [jnp.transpose(ref[pl.ds(n, F, stride=pitch), :]) for ref in (real_ref, imag_ref)]
        high, low = split(jnp.concatenate(both, axis=1))
        rows.append(jnp.concatenate((high, low, high), axis=1))
    out_ref[...] = dot_nn(jnp.concatenate(rows), table).reshape(per, channels, lags)


def correlate(j, previous, shard, own, other, blocks, samples, sources):
    size, lanes = blocks[0].shape
    shards = len(blocks)
    channels = own[0].shape[1]
    per = 16
    steps = size // per
    pitch = size + 8
    high, low = split_const(inverse_table(samples))
    operands = [*own, *other, high, low, *blocks]
    in_specs = [whole(x.shape) for x in operands]
    aliases = {}
    if previous is not None:
        aliases = {1 + len(operands): 0}
        operands.append(previous)
        in_specs.append(pl.BlockSpec(memory_space=pl.ANY))
    return pl.pallas_call(
        functools.partial(stack_kernel, shards=shards, pitch=pitch),
        grid_spec=pltpu.PrefetchScalarGridSpec(
            num_scalar_prefetch=1,
            grid=(steps,),
            in_specs=in_specs,
            out_specs=pl.BlockSpec((per, channels, LAGS), lambda s, p: (j * steps + s, 0, 0)),
            scratch_shapes=[
                pltpu.VMEM((F * pitch, channels), F32),
                pltpu.VMEM((F * pitch, channels), F32),
                pltpu.VMEM((shards, size, lanes), F32),
            ],
        ),
        out_shape=jax.ShapeDtypeStruct((sources, channels, LAGS), F32),
        input_output_aliases=aliases,
        compiler_params=pltpu.CompilerParams(vmem_limit_bytes=48 * 2**20, dimension_semantics=("arbitrary",)),
        cost_estimate=pl.CostEstimate(flops=20 * 10**9 // CHUNKS, bytes_accessed=48 * 2**20 // CHUNKS, transcendentals=0),
        name="stack_lags",
    )(shard[None], *operands)


def swap(x, axis, bits):
    return lax.ppermute(x, axis, [(i, i ^ bits) for i in range(lax.axis_size(axis))])


def body(recording, source_channels):
    segs, channels, samples = recording.shape
    shards = lax.axis_size("shard")
    shard, half = lax.axis_index("shard"), lax.axis_index("half")
    nsrc = source_channels.shape[0]
    row = source_channels[None, :]
    first, second, held = forward(recording, row, shard, shards)
    other_first = swap(first, "half", 1)

    got = lax.all_to_all(held, "shard", split_axis=0, concat_axis=0, tiled=True)
    mine = in_order(got.reshape(-1, got.shape[2]), row, shard, half, channels)
    counts = jnp.sum(source_channels[:, None] // channels == jnp.arange(shards)[None, :], axis=0)
    mine = lax.cond(
        jnp.max(counts) > CAP,
        lambda m: any_order(jnp.concatenate((first, second)), source_channels, half, shards),
        lambda m: list(m),
        list(mine),
    )
    other_first, *crossing = lax.optimization_barrier((other_first, *mine[CHUNKS:]))
    crossed = [swap(x, "half", 1) for x in crossing]
    second, *crossed = lax.optimization_barrier((second, *crossed))
    own, other = (first, second), (other_first, swap(second, "half", 1))

    result = None
    for j in range(CHUNKS):
        blocks = {0: pair_halves(mine[j], crossed[j], 2 * segs)}
        for k in range(1, shards // 4):
            blocks[4 * k] = swap(blocks[0], "shard", 4 * k)
        for bit in (2, 1):
            for r, x in list(blocks.items()):
                blocks[r ^ bit] = swap(x, "shard", bit)
        group = [blocks[r] for r in range(shards)]
        result = correlate(j, result, shard, own, other, group, samples, nsrc // 2)
    return result


def plain_forward_table(samples, freq_count):
    table = forward_table(samples)
    return jnp.stack((table[:freq_count], table[freq_count:]), axis=1)


def plain_inverse_table(samples, freq_count):
    table = inverse_table(samples)
    return jnp.stack((table[:freq_count], table[freq_count:]), axis=1)


def plain_whiten(spectra):
    magnitude = jnp.sqrt(spectra[:, 0] * spectra[:, 0] + spectra[:, 1] * spectra[:, 1])
    freq_count = magnitude.shape[0]
    padded = jnp.pad(magnitude, ((SMOOTH, SMOOTH), (0, 0), (0, 0)))
    smoothed = padded[0:freq_count]
    for offset in range(1, 2 * SMOOTH + 1):
        smoothed = smoothed + padded[offset : offset + freq_count]
    smoothed = smoothed / (2 * SMOOTH + 1)
    water_mark = jnp.mean(magnitude, axis=0, keepdims=True)
    divisor = smoothed + water_level * water_mark + epsilon
    return spectra / divisor[:, None]


def plain_correlate(whitened, indices):
    sources = jnp.take(whitened, indices, axis=2)
    src_real, src_imag = (sources[:, 0], sources[:, 1])
    rec_real, rec_imag = (whitened[:, 0], whitened[:, 1])
    high = lax.Precision.HIGHEST
    cross_real = jnp.einsum("fnx,fcx->fnc", src_real, rec_real, precision=high) + jnp.einsum(
        "fnx,fcx->fnc", src_imag, rec_imag, precision=high
    )
    cross_imag = jnp.einsum("fnx,fcx->fnc", src_real, rec_imag, precision=high) - jnp.einsum(
        "fnx,fcx->fnc", src_imag, rec_real, precision=high
    )
    return jnp.stack((cross_real, cross_imag), axis=1)


def plain_body(recording, source_channels):
    samples = recording.shape[2]
    high = lax.Precision.HIGHEST
    spectra = jnp.einsum("fqt,sct->fqcs", plain_forward_table(samples, F), recording, precision=high)
    whitened = plain_whiten(spectra)
    by_freq = lax.all_to_all(whitened, "shard", split_axis=0, concat_axis=2, tiled=True)
    per_half = source_channels.shape[0] // lax.axis_size("half")
    own_sources = lax.dynamic_slice_in_dim(source_channels, lax.axis_index("half") * per_half, per_half)
    combined = jnp.concatenate((by_freq, swap(by_freq, "half", 1)), axis=3)
    cross = plain_correlate(combined, own_sources)
    cross = lax.all_to_all(cross, "shard", split_axis=3, concat_axis=0, tiled=True)
    return jnp.einsum("fqnc,fql->ncl", cross, plain_inverse_table(samples, F), precision=high)


def solution(mesh):
    def run(recording, source_channels):
        shards = lax.axis_size("shard")
        fits = recording.shape[1] % 128 == 0 and shards == 16
        return (body if fits else plain_body)(recording, source_channels)

    return jax.shard_map(
        run,
        mesh=mesh,
        in_specs=(P("half", "shard", None), P()),
        out_specs=P("half", "shard", None),
        check_vma=False,
    )
```

```python
import functools

import jax
import jax.numpy as jnp
import numpy as np
from jax import lax
from jax.experimental import pallas as pl
from jax.experimental.pallas import tpu as pltpu
from jax.sharding import PartitionSpec as P

F = 128
LAGS = 512
SMOOTH = 2
SEG = 32
CHUNKS = 1
CAP = 32

water_level = 0.2
epsilon = 1e-05

BF16 = jnp.bfloat16
F32 = jnp.float32


def forward_table(samples):
    bins = np.arange(F, dtype=np.int64) + 1
    times = np.arange(samples, dtype=np.int64)
    angle = 2.0 * np.pi * (bins[:, None] * times[None, :] % samples) / samples
    taper = 0.5 - 0.5 * np.cos(2.0 * np.pi * times / samples)
    return np.concatenate((np.cos(angle) * taper, -np.sin(angle) * taper)).astype(np.float32)


def inverse_table(samples):
    bins = np.arange(F, dtype=np.int64) + 1
    shifts = np.arange(LAGS, dtype=np.int64) - LAGS // 2
    angle = 2.0 * np.pi * (bins[:, None] * shifts[None, :] % samples) / samples
    scale = 1.0 / np.sqrt(float(SEG * F))
    return np.concatenate((np.cos(angle) * scale, -np.sin(angle) * scale)).astype(np.float32)


def split_const(table):
    high = table.astype(jnp.bfloat16)
    low = (table - high.astype(np.float32)).astype(jnp.bfloat16)
    return high, low


def split(x):
    high = x.astype(BF16)
    low = (x - high.astype(F32)).astype(BF16)
    return high, low


def dot_nt(a, b):
    return lax.dot_general(a, b, (((1,), (1,)), ((), ())), preferred_element_type=F32)


def dot_nn(a, b):
    return lax.dot_general(a, b, (((1,), (0,)), ((), ())), preferred_element_type=F32)


def whiten_tile(real, imag):
    magnitude = jnp.sqrt(real * real + imag * imag)
    row = lax.broadcasted_iota(jnp.int32, magnitude.shape, 0)
    smoothed = magnitude
    for offset in range(1, SMOOTH + 1):
        smoothed = smoothed + jnp.where(row >= offset, pltpu.roll(magnitude, offset, 0), 0.0)
        smoothed = smoothed + jnp.where(row < F - offset, pltpu.roll(magnitude, F - offset, 0), 0.0)
    water_mark = jnp.mean(magnitude, axis=0, keepdims=True)
    divisor = smoothed * (1.0 / (2 * SMOOTH + 1)) + water_level * water_mark + epsilon
    return real / divisor, imag / divisor


def as_column(row):
    n = row.shape[1]
    here = lax.broadcasted_iota(jnp.int32, (n, n), 0) == lax.broadcasted_iota(jnp.int32, (n, n), 1)
    return jnp.sum(jnp.where(here, row.astype(F32), 0.0), axis=1, keepdims=True).astype(jnp.int32)


def ranks(col, row, channels, axis):
    same = col // channels == row // channels
    first = lax.broadcasted_iota(jnp.int32, same.shape, axis) < lax.broadcasted_iota(jnp.int32, same.shape, 1 - axis)
    return jnp.sum(jnp.where(same & first, 1.0, 0.0), axis=axis, keepdims=True).astype(jnp.int32)


def spectra_kernel(place_ref, rec_ref, hi_ref, lo_ref, row_ref, first_ref, second_ref, held_ref, *, segs):
    step = pl.program_id(0)
    per, channels, samples = rec_ref.shape
    high, low = split(rec_ref[...].reshape(per * channels, samples))
    spectra = dot_nt(hi_ref[...], high) + (dot_nt(lo_ref[...], high) + dot_nt(hi_ref[...], low))
    for i in range(per):
        lanes = slice(i * channels, (i + 1) * channels)
        real, imag = whiten_tile(spectra[:F, lanes], spectra[F:, lanes])
        seg = step * per + i
        for ref, start in ((first_ref, 0), (second_ref, first_ref.shape[0] // (2 * segs))):
            count = ref.shape[0] // (2 * segs)
            ref[pl.ds(seg, count, stride=2 * segs), :] = real[start : start + count]
            ref[pl.ds(seg + segs, count, stride=2 * segs), :] = imag[start : start + count]

    @pl.when(step == pl.num_programs(0) - 1)
    def _():
        shards, cap, rows = held_ref.shape
        shard = place_ref[0]
        row = row_ref[...]
        col = as_column(row)
        nsrc = col.shape[0]
        rank = jnp.where(row // channels == shard, ranks(col, row, channels, 0), -1)
        chosen = (lax.broadcasted_iota(jnp.int32, (cap, nsrc), 0) == rank).astype(F32).astype(BF16)
        lane = lax.broadcasted_iota(jnp.int32, (nsrc, channels), 1)
        where = (col - shard * channels == lane).astype(F32).astype(BF16)
        hot = dot_nn(chosen, where).astype(BF16)
        hot = jnp.concatenate((hot, hot), axis=1)
        for d in range(shards):
            cut = first_ref.shape[0] // rows
            ref, at = (first_ref, d) if d < cut else (second_ref, d - cut)
            high, low = split(ref[at * rows : (at + 1) * rows, :])
            held_ref[d] = dot_nt(hot, jnp.concatenate((high, low), axis=1))


def whole(shape):
    return pl.BlockSpec(shape, lambda *_: (0,) * len(shape))


def first_blocks(shards):
    return 5 * shards // 16


def forward(recording, row, shard, shards):
    segs, channels, samples = recording.shape
    per = 4
    nsrc = row.shape[1]
    rows = F // shards * 2 * segs
    held = (shards, CAP, rows)
    cut = first_blocks(shards)
    white = [(cut * rows, channels), ((shards - cut) * rows, channels)]
    high, low = split_const(forward_table(samples))
    return pl.pallas_call(
        functools.partial(spectra_kernel, segs=segs),
        grid_spec=pltpu.PrefetchScalarGridSpec(
            num_scalar_prefetch=1,
            grid=(segs // per,),
            in_specs=[
                pl.BlockSpec((per, channels, samples), lambda s, p: (s, 0, 0)),
                whole((2 * F, samples)),
                whole((2 * F, samples)),
                whole((1, nsrc)),
            ],
            out_specs=[whole(x) for x in (*white, held)],
        ),
        out_shape=[jax.ShapeDtypeStruct(x, F32) for x in (*white, held)],
        compiler_params=pltpu.CompilerParams(vmem_limit_bytes=60 * 2**20, dimension_semantics=("arbitrary",)),
        cost_estimate=pl.CostEstimate(flops=6 * 10**9, bytes_accessed=16 * 2**20, transcendentals=0),
        name="forward_whiten",
    )(shard[None], recording, high, low, row)


def order_kernel(place_ref, got_ref, row_ref, *outs, channels):
    row = row_ref[...]
    col = as_column(row)
    nsrc = col.shape[0]
    entries = got_ref.shape[0]
    at = col // channels * CAP + ranks(col, row, channels, 1)
    hot = (at == lax.broadcasted_iota(jnp.int32, (nsrc, entries), 1)).astype(F32).astype(BF16)
    high, low = split(got_ref[...])
    rows = dot_nn(hot, high) + dot_nn(hot, low)
    size = outs[0].shape[0]
    per_half = nsrc // 2
    for h in range(2):

        @pl.when(place_ref[1] == h)
        def _():
            for k, out in enumerate(outs):
                start = ((k // CHUNKS) ^ h) * per_half + k % CHUNKS * size
                out[...] = rows[start : start + size]


def in_order(got, row, shard, half, channels):
    nsrc = row.shape[1]
    size = nsrc // 2 // CHUNKS
    shape = (size, got.shape[1])
    return pl.pallas_call(
        functools.partial(order_kernel, channels=channels),
        grid_spec=pltpu.PrefetchScalarGridSpec(
            num_scalar_prefetch=1,
            grid=(1,),
            in_specs=[whole(got.shape), whole((1, nsrc))],
            out_specs=[whole(shape)] * (2 * CHUNKS),
        ),
        out_shape=[jax.ShapeDtypeStruct(shape, F32)] * (2 * CHUNKS),
        compiler_params=pltpu.CompilerParams(vmem_limit_bytes=16 * 2**20),
        cost_estimate=pl.CostEstimate(flops=10**8, bytes_accessed=2**20, transcendentals=0),
        name="order_sources",
    )(jnp.stack((shard, half)), got, row)


def any_order(white, source_channels, half, shards):
    channels = white.shape[1]
    bins = white.reshape(shards, -1, channels)
    bins = lax.all_to_all(bins, "shard", split_axis=0, concat_axis=2, tiled=True)[0]
    rows = jnp.take(bins, source_channels, axis=1).T
    per_half = rows.shape[0] // 2
    mine = lax.dynamic_slice_in_dim(rows, half * per_half, per_half)
    others = lax.dynamic_slice_in_dim(rows, (1 - half) * per_half, per_half)
    return [*jnp.split(mine, CHUNKS), *jnp.split(others, CHUNKS)]


def stack_kernel(place_ref, own0_ref, own1_ref, oth0_ref, oth1_ref, hi_ref, lo_ref, *refs, stacked, pitch):
    stacks = refs[: len(stacked)]
    out_ref, real_ref, imag_ref, src_ref = refs[-4:]
    step = pl.program_id(0)
    per, channels, lags = out_ref.shape
    _, shards, size, lanes = src_ref.shape
    bins = F // shards
    width = lanes // bins
    segs = width // 2
    cut = own0_ref.shape[0] // (bins * width)

    def turn(v):
        return jnp.concatenate((v[segs:], -v[:segs]))

    def block(owner, own_ref, oth_ref, skip):
        for group in range(0, bins, 4):
            lanes = slice(group * width, (group + 4) * width)
            source = [split(src_ref[h, place_ref[0] ^ owner, :, lanes]) for h in range(2)]
            for i in range(group, group + 4):
                rows = pl.ds(pl.multiple_of(((owner - skip) * bins + i) * width, width), width)
                (ah, al), (bh, bl) = split(own_ref[rows, :]), split(oth_ref[rows, :])
                right = (ah, bh, ah, bh, al, bl)
                rhs = jnp.concatenate((jnp.concatenate(right), jnp.concatenate([turn(v) for v in right])), axis=1)
                at = slice((i - group) * width, (i - group + 1) * width)
                (ah, al), (bh, bl) = source
                lhs = jnp.concatenate([v[:, at] for v in (ah, bh, al, bl, ah, bh)], axis=1)
                cross = dot_nn(lhs, rhs)
                to = pl.ds(pl.multiple_of((owner * bins + i) * pitch, 8), size)
                real_ref[to, :] = cross[:, :channels]
                imag_ref[to, :] = cross[:, channels:]

    @pl.when(step == 0)
    def _():
        for held, ref in zip(stacked, stacks):
            for k, (h, r) in enumerate(held):
                src_ref[h, r] = ref[k]

        def first(owner, carry):
            block(owner, own0_ref, oth0_ref, 0)
            return carry

        def second(owner, carry):
            block(owner, own1_ref, oth1_ref, cut)
            return carry

        lax.fori_loop(0, cut, first, 0, unroll=4)
        lax.fori_loop(cut, shards, second, 0, unroll=4)

    table = jnp.concatenate((hi_ref[...], hi_ref[...], lo_ref[...]))
    rows = []
    for i in range(per):
        n = step * per + i
        both = [jnp.transpose(ref[pl.ds(n, F, stride=pitch), :]) for ref in (real_ref, imag_ref)]
        high, low = split(jnp.concatenate(both, axis=1))
        rows.append(jnp.concatenate((high, low, high), axis=1))
    out_ref[...] = dot_nn(jnp.concatenate(rows), table).reshape(per, channels, lags)


def correlate(j, previous, shard, own, other, stacks, samples, sources):
    stacked = [held for held, _ in stacks]
    shards = sum(map(len, stacked)) // 2
    size, lanes = stacks[0][1].shape[1:]
    channels = own[0].shape[1]
    per = 16
    steps = size // per
    pitch = size + 8
    high, low = split_const(inverse_table(samples))
    operands = [*own, *other, high, low, *(x for _, x in stacks)]
    in_specs = [whole(x.shape) for x in operands]
    aliases = {}
    if previous is not None:
        aliases = {1 + len(operands): 0}
        operands.append(previous)
        in_specs.append(pl.BlockSpec(memory_space=pl.ANY))
    return pl.pallas_call(
        functools.partial(stack_kernel, stacked=stacked, pitch=pitch),
        grid_spec=pltpu.PrefetchScalarGridSpec(
            num_scalar_prefetch=1,
            grid=(steps,),
            in_specs=in_specs,
            out_specs=pl.BlockSpec((per, channels, LAGS), lambda s, p: (j * steps + s, 0, 0)),
            scratch_shapes=[
                pltpu.VMEM((F * pitch, channels), F32),
                pltpu.VMEM((F * pitch, channels), F32),
                pltpu.VMEM((2, shards, size, lanes), F32),
            ],
        ),
        out_shape=jax.ShapeDtypeStruct((sources, channels, LAGS), F32),
        input_output_aliases=aliases,
        compiler_params=pltpu.CompilerParams(vmem_limit_bytes=36 * 2**20, dimension_semantics=("arbitrary",)),
        cost_estimate=pl.CostEstimate(flops=20 * 10**9 // CHUNKS, bytes_accessed=48 * 2**20 // CHUNKS, transcendentals=0),
        name="stack_lags",
    )(shard[None], *operands)


def swap(x, axis, bits):
    return lax.ppermute(x, axis, [(i, i ^ bits) for i in range(lax.axis_size(axis))])


def gather(own, crossing, passed):
    crossing, passed = lax.optimization_barrier((crossing, passed))
    other = swap(crossing, "half", 1)
    first = [swap(own, "shard", r) for r in (8, 4, 2)]
    *first, after = lax.optimization_barrier((*first, other))
    second = [swap(after, "shard", r) for r in (8, 4, 2)]
    *two, own, after = lax.optimization_barrier((*first, *second, own, after))
    first, second = two[:3], two[3:]
    mine = jnp.stack((own, after))
    line = jnp.stack((first[0], second[0], first[1], second[1]))
    far = swap(mine, "shard", 12)
    across = swap(line, "shard", 2)
    far_across = swap(far, "shard", 2)
    stacks = []
    for relative, blocks in (
        ((8, 4), line),
        ((0, 2), jnp.concatenate((mine, jnp.stack((first[2], second[2]))))),
        ((10, 6), across),
        ((12, 14), jnp.concatenate((far, far_across))),
    ):
        held = [(h, r) for r in relative for h in range(2)]
        stacks += [(held, blocks), ([(h, r + 1) for h, r in held], swap(blocks, "shard", 1))]
    return stacks, passed, other


def body(recording, source_channels):
    segs, channels, samples = recording.shape
    shards = lax.axis_size("shard")
    shard, half = lax.axis_index("shard"), lax.axis_index("half")
    nsrc = source_channels.shape[0]
    row = source_channels[None, :]
    first, second, held = forward(recording, row, shard, shards)
    other_first = swap(first, "half", 1)

    got = lax.all_to_all(held, "shard", split_axis=0, concat_axis=0, tiled=True)
    mine = in_order(got.reshape(-1, got.shape[2]), row, shard, half, channels)
    counts = jnp.sum(source_channels[:, None] // channels == jnp.arange(shards)[None, :], axis=0)
    mine = lax.cond(
        jnp.max(counts) > CAP,
        lambda m: any_order(jnp.concatenate((first, second)), source_channels, half, shards),
        lambda m: list(m),
        list(mine),
    )
    stacks, other_first, crossed = gather(mine[0], mine[1], other_first)
    second, crossed = lax.optimization_barrier((second, crossed))
    own, other = (first, second), (other_first, swap(second, "half", 1))
    return correlate(0, None, shard, own, other, stacks, samples, nsrc // 2)


def plain_forward_table(samples, freq_count):
    table = forward_table(samples)
    return jnp.stack((table[:freq_count], table[freq_count:]), axis=1)


def plain_inverse_table(samples, freq_count):
    table = inverse_table(samples)
    return jnp.stack((table[:freq_count], table[freq_count:]), axis=1)


def plain_whiten(spectra):
    magnitude = jnp.sqrt(spectra[:, 0] * spectra[:, 0] + spectra[:, 1] * spectra[:, 1])
    freq_count = magnitude.shape[0]
    padded = jnp.pad(magnitude, ((SMOOTH, SMOOTH), (0, 0), (0, 0)))
    smoothed = padded[0:freq_count]
    for offset in range(1, 2 * SMOOTH + 1):
        smoothed = smoothed + padded[offset : offset + freq_count]
    smoothed = smoothed / (2 * SMOOTH + 1)
    water_mark = jnp.mean(magnitude, axis=0, keepdims=True)
    divisor = smoothed + water_level * water_mark + epsilon
    return spectra / divisor[:, None]


def plain_correlate(whitened, indices):
    sources = jnp.take(whitened, indices, axis=2)
    src_real, src_imag = (sources[:, 0], sources[:, 1])
    rec_real, rec_imag = (whitened[:, 0], whitened[:, 1])
    high = lax.Precision.HIGHEST
    cross_real = jnp.einsum("fnx,fcx->fnc", src_real, rec_real, precision=high) + jnp.einsum(
        "fnx,fcx->fnc", src_imag, rec_imag, precision=high
    )
    cross_imag = jnp.einsum("fnx,fcx->fnc", src_real, rec_imag, precision=high) - jnp.einsum(
        "fnx,fcx->fnc", src_imag, rec_real, precision=high
    )
    return jnp.stack((cross_real, cross_imag), axis=1)


def plain_body(recording, source_channels):
    samples = recording.shape[2]
    high = lax.Precision.HIGHEST
    spectra = jnp.einsum("fqt,sct->fqcs", plain_forward_table(samples, F), recording, precision=high)
    whitened = plain_whiten(spectra)
    by_freq = lax.all_to_all(whitened, "shard", split_axis=0, concat_axis=2, tiled=True)
    per_half = source_channels.shape[0] // lax.axis_size("half")
    own_sources = lax.dynamic_slice_in_dim(source_channels, lax.axis_index("half") * per_half, per_half)
    combined = jnp.concatenate((by_freq, swap(by_freq, "half", 1)), axis=3)
    cross = plain_correlate(combined, own_sources)
    cross = lax.all_to_all(cross, "shard", split_axis=3, concat_axis=0, tiled=True)
    return jnp.einsum("fqnc,fql->ncl", cross, plain_inverse_table(samples, F), precision=high)


def solution(mesh):
    def run(recording, source_channels):
        shards = lax.axis_size("shard")
        fits = recording.shape[1] % 128 == 0 and shards == 16
        return (body if fits else plain_body)(recording, source_channels)

    return jax.shard_map(
        run,
        mesh=mesh,
        in_specs=(P("half", "shard", None), P()),
        out_specs=P("half", "shard", None),
        check_vma=False,
    )
```

```python
import functools

import jax
import jax.numpy as jnp
import numpy as np
from jax import lax
from jax.experimental import pallas as pl
from jax.experimental.pallas import tpu as pltpu
from jax.sharding import PartitionSpec as P

F = 128
LAGS = 512
SMOOTH = 2
SEG = 32
CHUNKS = 1
CAP = 32

water_level = 0.2
epsilon = 1e-05

BF16 = jnp.bfloat16
F32 = jnp.float32


def forward_table(samples):
    bins = np.arange(F, dtype=np.int64) + 1
    times = np.arange(samples, dtype=np.int64)
    angle = 2.0 * np.pi * (bins[:, None] * times[None, :] % samples) / samples
    taper = 0.5 - 0.5 * np.cos(2.0 * np.pi * times / samples)
    return np.concatenate((np.cos(angle) * taper, -np.sin(angle) * taper)).T.astype(np.float32)


def inverse_table(samples):
    bins = np.arange(F, dtype=np.int64) + 1
    shifts = np.arange(LAGS, dtype=np.int64) - LAGS // 2
    angle = 2.0 * np.pi * (bins[:, None] * shifts[None, :] % samples) / samples
    scale = 1.0 / np.sqrt(float(SEG * F))
    return np.concatenate((np.cos(angle) * scale, -np.sin(angle) * scale)).astype(np.float32)


def split_const(table):
    high = table.astype(jnp.bfloat16)
    low = (table - high.astype(np.float32)).astype(jnp.bfloat16)
    return high, low


def split(x):
    high = x.astype(BF16)
    low = (x - high.astype(F32)).astype(BF16)
    return high, low


def dot_nt(a, b):
    return lax.dot_general(a, b, (((1,), (1,)), ((), ())), preferred_element_type=F32)


def dot_nn(a, b):
    return lax.dot_general(a, b, (((1,), (0,)), ((), ())), preferred_element_type=F32)


def whiten_tile(real, imag):
    magnitude = jnp.sqrt(real * real + imag * imag)
    row = lax.broadcasted_iota(jnp.int32, magnitude.shape, 0)
    smoothed = magnitude
    for offset in range(1, SMOOTH + 1):
        smoothed = smoothed + jnp.where(row >= offset, pltpu.roll(magnitude, offset, 0), 0.0)
        smoothed = smoothed + jnp.where(row < F - offset, pltpu.roll(magnitude, F - offset, 0), 0.0)
    water_mark = jnp.mean(magnitude, axis=0, keepdims=True)
    divisor = smoothed * (1.0 / (2 * SMOOTH + 1)) + water_level * water_mark + epsilon
    return real / divisor, imag / divisor


def as_column(row):
    n = row.shape[1]
    here = lax.broadcasted_iota(jnp.int32, (n, n), 0) == lax.broadcasted_iota(jnp.int32, (n, n), 1)
    return jnp.sum(jnp.where(here, row.astype(F32), 0.0), axis=1, keepdims=True).astype(jnp.int32)


def ranks(col, row, channels, axis):
    same = col // channels == row // channels
    first = lax.broadcasted_iota(jnp.int32, same.shape, axis) < lax.broadcasted_iota(jnp.int32, same.shape, 1 - axis)
    return jnp.sum(jnp.where(same & first, 1.0, 0.0), axis=axis, keepdims=True).astype(jnp.int32)


def spectra_kernel(place_ref, rec_ref, hi_ref, lo_ref, row_ref, first_ref, second_ref, held_ref, *, segs):
    step = pl.program_id(0)
    per, channels, samples = rec_ref.shape
    for i in range(per):
        high, low = split(rec_ref[i])
        spectra = dot_nn(high, hi_ref[...]) + (dot_nn(low, hi_ref[...]) + dot_nn(high, lo_ref[...]))
        real, imag = whiten_tile(jnp.transpose(spectra[:, :F]), jnp.transpose(spectra[:, F:]))
        seg = step * per + i
        for ref, start in ((first_ref, 0), (second_ref, first_ref.shape[0] // (2 * segs))):
            count = ref.shape[0] // (2 * segs)
            ref[pl.ds(seg, count, stride=2 * segs), :] = real[start : start + count]
            ref[pl.ds(seg + segs, count, stride=2 * segs), :] = imag[start : start + count]

    @pl.when(step == pl.num_programs(0) - 1)
    def _():
        shards, cap, rows = held_ref.shape
        shard = place_ref[0]
        row = row_ref[...]
        col = as_column(row)
        nsrc = col.shape[0]
        rank = jnp.where(row // channels == shard, ranks(col, row, channels, 0), -1)
        chosen = (lax.broadcasted_iota(jnp.int32, (cap, nsrc), 0) == rank).astype(F32).astype(BF16)
        lane = lax.broadcasted_iota(jnp.int32, (nsrc, channels), 1)
        where = (col - shard * channels == lane).astype(F32).astype(BF16)
        hot = dot_nn(chosen, where).astype(BF16)
        hot = jnp.concatenate((hot, hot), axis=1)
        for d in range(shards):
            cut = first_ref.shape[0] // rows
            ref, at = (first_ref, d) if d < cut else (second_ref, d - cut)
            high, low = split(ref[at * rows : (at + 1) * rows, :])
            held_ref[d] = dot_nt(hot, jnp.concatenate((high, low), axis=1))


def whole(shape):
    return pl.BlockSpec(shape, lambda *_: (0,) * len(shape))


def first_blocks(shards):
    return 5 * shards // 16


def forward(recording, row, shard, shards):
    segs, channels, samples = recording.shape
    per = 4
    nsrc = row.shape[1]
    rows = F // shards * 2 * segs
    held = (shards, CAP, rows)
    cut = first_blocks(shards)
    white = [(cut * rows, channels), ((shards - cut) * rows, channels)]
    high, low = split_const(forward_table(samples))
    return pl.pallas_call(
        functools.partial(spectra_kernel, segs=segs),
        grid_spec=pltpu.PrefetchScalarGridSpec(
            num_scalar_prefetch=1,
            grid=(segs // per,),
            in_specs=[
                pl.BlockSpec((per, channels, samples), lambda s, p: (s, 0, 0)),
                whole((samples, 2 * F)),
                whole((samples, 2 * F)),
                whole((1, nsrc)),
            ],
            out_specs=[whole(x) for x in (*white, held)],
        ),
        out_shape=[jax.ShapeDtypeStruct(x, F32) for x in (*white, held)],
        compiler_params=pltpu.CompilerParams(vmem_limit_bytes=60 * 2**20, dimension_semantics=("arbitrary",)),
        cost_estimate=pl.CostEstimate(flops=6 * 10**9, bytes_accessed=16 * 2**20, transcendentals=0),
        name="forward_whiten",
    )(shard[None], recording, high, low, row)


def order_kernel(place_ref, got_ref, row_ref, *outs, channels):
    row = row_ref[...]
    col = as_column(row)
    nsrc = col.shape[0]
    entries = got_ref.shape[0]
    at = col // channels * CAP + ranks(col, row, channels, 1)
    hot = (at == lax.broadcasted_iota(jnp.int32, (nsrc, entries), 1)).astype(F32).astype(BF16)
    high, low = split(got_ref[...])
    rows = dot_nn(hot, high) + dot_nn(hot, low)
    size = outs[0].shape[0]
    per_half = nsrc // 2
    for h in range(2):

        @pl.when(place_ref[1] == h)
        def _():
            for k, out in enumerate(outs):
                start = ((k // CHUNKS) ^ h) * per_half + k % CHUNKS * size
                out[...] = rows[start : start + size]


def in_order(got, row, shard, half, channels):
    nsrc = row.shape[1]
    size = nsrc // 2 // CHUNKS
    shape = (size, got.shape[1])
    return pl.pallas_call(
        functools.partial(order_kernel, channels=channels),
        grid_spec=pltpu.PrefetchScalarGridSpec(
            num_scalar_prefetch=1,
            grid=(1,),
            in_specs=[whole(got.shape), whole((1, nsrc))],
            out_specs=[whole(shape)] * (2 * CHUNKS),
        ),
        out_shape=[jax.ShapeDtypeStruct(shape, F32)] * (2 * CHUNKS),
        compiler_params=pltpu.CompilerParams(vmem_limit_bytes=16 * 2**20),
        cost_estimate=pl.CostEstimate(flops=10**8, bytes_accessed=2**20, transcendentals=0),
        name="order_sources",
    )(jnp.stack((shard, half)), got, row)


def any_order(white, source_channels, half, shards):
    channels = white.shape[1]
    bins = white.reshape(shards, -1, channels)
    bins = lax.all_to_all(bins, "shard", split_axis=0, concat_axis=2, tiled=True)[0]
    rows = jnp.take(bins, source_channels, axis=1).T
    per_half = rows.shape[0] // 2
    mine = lax.dynamic_slice_in_dim(rows, half * per_half, per_half)
    others = lax.dynamic_slice_in_dim(rows, (1 - half) * per_half, per_half)
    return [*jnp.split(mine, CHUNKS), *jnp.split(others, CHUNKS)]


def stack_kernel(place_ref, own0_ref, own1_ref, oth0_ref, oth1_ref, hi_ref, lo_ref, *refs, stacked, pitch):
    stacks = refs[: len(stacked)]
    out_ref, real_ref, imag_ref, src_ref = refs[-4:]
    step = pl.program_id(0)
    per, channels, lags = out_ref.shape
    _, shards, size, lanes = src_ref.shape
    bins = F // shards
    width = lanes // bins
    segs = width // 2
    cut = own0_ref.shape[0] // (bins * width)

    def turn(v):
        return jnp.concatenate((v[segs:], -v[:segs]))

    def block(owner, own_ref, oth_ref, skip):
        for group in range(0, bins, 4):
            lanes = slice(group * width, (group + 4) * width)
            source = [split(src_ref[h, place_ref[0] ^ owner, :, lanes]) for h in range(2)]
            for i in range(group, group + 4):
                rows = pl.ds(pl.multiple_of(((owner - skip) * bins + i) * width, width), width)
                (ah, al), (bh, bl) = split(own_ref[rows, :]), split(oth_ref[rows, :])
                right = (ah, bh, ah, bh, al, bl)
                rhs = jnp.concatenate((jnp.concatenate(right), jnp.concatenate([turn(v) for v in right])), axis=1)
                at = slice((i - group) * width, (i - group + 1) * width)
                (ah, al), (bh, bl) = source
                lhs = jnp.concatenate([v[:, at] for v in (ah, bh, al, bl, ah, bh)], axis=1)
                cross = dot_nn(lhs, rhs)
                to = pl.ds(pl.multiple_of((owner * bins + i) * pitch, 8), size)
                real_ref[to, :] = cross[:, :channels]
                imag_ref[to, :] = cross[:, channels:]

    @pl.when(step == 0)
    def _():
        for held, ref in zip(stacked, stacks):
            for k, (h, r) in enumerate(held):
                src_ref[h, r] = ref[k]

        def four(group, carry, parts):
            for k, (own_ref, oth_ref, skip) in enumerate(parts):
                block(4 * group + k, own_ref, oth_ref, skip)
            return carry

        for group in range(shards // 4):
            parts = [
                (own0_ref, oth0_ref, 0) if owner < cut else (own1_ref, oth1_ref, cut)
                for owner in range(4 * group, 4 * group + 4)
            ]
            lax.fori_loop(group, group + 1, functools.partial(four, parts=parts), 0)

    table = jnp.concatenate((hi_ref[...], hi_ref[...], lo_ref[...]))
    rows = []
    for i in range(per):
        n = step * per + i
        both = [jnp.transpose(ref[pl.ds(n, F, stride=pitch), :]) for ref in (real_ref, imag_ref)]
        high, low = split(jnp.concatenate(both, axis=1))
        rows.append(jnp.concatenate((high, low, high), axis=1))
    out_ref[...] = dot_nn(jnp.concatenate(rows), table).reshape(per, channels, lags)


def correlate(j, previous, shard, own, other, stacks, samples, sources):
    stacked = [held for held, _ in stacks]
    shards = sum(map(len, stacked)) // 2
    size, lanes = stacks[0][1].shape[1:]
    channels = own[0].shape[1]
    per = 16
    steps = size // per
    pitch = size + 8
    high, low = split_const(inverse_table(samples))
    operands = [*own, *other, high, low, *(x for _, x in stacks)]
    in_specs = [whole(x.shape) for x in operands]
    aliases = {}
    if previous is not None:
        aliases = {1 + len(operands): 0}
        operands.append(previous)
        in_specs.append(pl.BlockSpec(memory_space=pl.ANY))
    return pl.pallas_call(
        functools.partial(stack_kernel, stacked=stacked, pitch=pitch),
        grid_spec=pltpu.PrefetchScalarGridSpec(
            num_scalar_prefetch=1,
            grid=(steps,),
            in_specs=in_specs,
            out_specs=pl.BlockSpec((per, channels, LAGS), lambda s, p: (j * steps + s, 0, 0)),
            scratch_shapes=[
                pltpu.VMEM((F * pitch, channels), F32),
                pltpu.VMEM((F * pitch, channels), F32),
                pltpu.VMEM((2, shards, size, lanes), F32),
            ],
        ),
        out_shape=jax.ShapeDtypeStruct((sources, channels, LAGS), F32),
        input_output_aliases=aliases,
        compiler_params=pltpu.CompilerParams(vmem_limit_bytes=36 * 2**20, dimension_semantics=("arbitrary",)),
        cost_estimate=pl.CostEstimate(flops=20 * 10**9 // CHUNKS, bytes_accessed=48 * 2**20 // CHUNKS, transcendentals=0),
        name="stack_lags",
    )(shard[None], *operands)


def swap(x, axis, bits):
    return lax.ppermute(x, axis, [(i, i ^ bits) for i in range(lax.axis_size(axis))])


def gather(own, crossing, passed):
    crossing, passed = lax.optimization_barrier((crossing, passed))
    other = swap(crossing, "half", 1)
    first = [swap(own, "shard", r) for r in (8, 4, 2)]
    *first, after = lax.optimization_barrier((*first, other))
    second = [swap(after, "shard", r) for r in (8, 4, 2)]
    *two, own, after = lax.optimization_barrier((*first, *second, own, after))
    first, second = two[:3], two[3:]
    mine = jnp.stack((own, after))
    line = jnp.stack((first[0], second[0], first[1], second[1]))
    far = swap(mine, "shard", 12)
    across = swap(line, "shard", 2)
    far, mine, line = lax.optimization_barrier((far, mine, line))
    far_across = swap(far, "shard", 2)
    stacks = []
    for relative, blocks in (
        ((8, 4), line),
        ((0, 2), jnp.concatenate((mine, jnp.stack((first[2], second[2]))))),
        ((10, 6), across),
        ((12, 14), jnp.concatenate((far, far_across))),
    ):
        held = [(h, r) for r in relative for h in range(2)]
        stacks += [(held, blocks), ([(h, r + 1) for h, r in held], swap(blocks, "shard", 1))]
    return stacks, passed, other


def body(recording, source_channels):
    segs, channels, samples = recording.shape
    shards = lax.axis_size("shard")
    shard, half = lax.axis_index("shard"), lax.axis_index("half")
    nsrc = source_channels.shape[0]
    row = source_channels[None, :]
    first, second, held = forward(recording, row, shard, shards)
    other_first = swap(first, "half", 1)

    got = lax.all_to_all(held, "shard", split_axis=0, concat_axis=0, tiled=True)
    mine = in_order(got.reshape(-1, got.shape[2]), row, shard, half, channels)
    counts = jnp.sum(source_channels[:, None] // channels == jnp.arange(shards)[None, :], axis=0)
    mine = lax.cond(
        jnp.max(counts) > CAP,
        lambda m: any_order(jnp.concatenate((first, second)), source_channels, half, shards),
        lambda m: list(m),
        list(mine),
    )
    stacks, other_first, crossed = gather(mine[0], mine[1], other_first)
    second, crossed = lax.optimization_barrier((second, crossed))
    own, other = (first, second), (other_first, swap(second, "half", 1))
    return correlate(0, None, shard, own, other, stacks, samples, nsrc // 2)


def plain_forward_table(samples, freq_count):
    table = forward_table(samples).T
    return jnp.stack((table[:freq_count], table[freq_count:]), axis=1)


def plain_inverse_table(samples, freq_count):
    table = inverse_table(samples)
    return jnp.stack((table[:freq_count], table[freq_count:]), axis=1)


def plain_whiten(spectra):
    magnitude = jnp.sqrt(spectra[:, 0] * spectra[:, 0] + spectra[:, 1] * spectra[:, 1])
    freq_count = magnitude.shape[0]
    padded = jnp.pad(magnitude, ((SMOOTH, SMOOTH), (0, 0), (0, 0)))
    smoothed = padded[0:freq_count]
    for offset in range(1, 2 * SMOOTH + 1):
        smoothed = smoothed + padded[offset : offset + freq_count]
    smoothed = smoothed / (2 * SMOOTH + 1)
    water_mark = jnp.mean(magnitude, axis=0, keepdims=True)
    divisor = smoothed + water_level * water_mark + epsilon
    return spectra / divisor[:, None]


def plain_correlate(whitened, indices):
    sources = jnp.take(whitened, indices, axis=2)
    src_real, src_imag = (sources[:, 0], sources[:, 1])
    rec_real, rec_imag = (whitened[:, 0], whitened[:, 1])
    high = lax.Precision.HIGHEST
    cross_real = jnp.einsum("fnx,fcx->fnc", src_real, rec_real, precision=high) + jnp.einsum(
        "fnx,fcx->fnc", src_imag, rec_imag, precision=high
    )
    cross_imag = jnp.einsum("fnx,fcx->fnc", src_real, rec_imag, precision=high) - jnp.einsum(
        "fnx,fcx->fnc", src_imag, rec_real, precision=high
    )
    return jnp.stack((cross_real, cross_imag), axis=1)


def plain_body(recording, source_channels):
    samples = recording.shape[2]
    high = lax.Precision.HIGHEST
    spectra = jnp.einsum("fqt,sct->fqcs", plain_forward_table(samples, F), recording, precision=high)
    whitened = plain_whiten(spectra)
    by_freq = lax.all_to_all(whitened, "shard", split_axis=0, concat_axis=2, tiled=True)
    per_half = source_channels.shape[0] // lax.axis_size("half")
    own_sources = lax.dynamic_slice_in_dim(source_channels, lax.axis_index("half") * per_half, per_half)
    combined = jnp.concatenate((by_freq, swap(by_freq, "half", 1)), axis=3)
    cross = plain_correlate(combined, own_sources)
    cross = lax.all_to_all(cross, "shard", split_axis=3, concat_axis=0, tiled=True)
    return jnp.einsum("fqnc,fql->ncl", cross, plain_inverse_table(samples, F), precision=high)


def solution(mesh):
    def run(recording, source_channels):
        shards = lax.axis_size("shard")
        fits = recording.shape[1] % 128 == 0 and shards == 16
        return (body if fits else plain_body)(recording, source_channels)

    return jax.shard_map(
        run,
        mesh=mesh,
        in_specs=(P("half", "shard", None), P()),
        out_specs=P("half", "shard", None),
        check_vma=False,
    )
```

```python
import functools

import jax
import jax.numpy as jnp
import numpy as np
from jax import lax
from jax.experimental import pallas as pl
from jax.experimental.pallas import tpu as pltpu
from jax.sharding import PartitionSpec as P

F = 128
LAGS = 512
SMOOTH = 2
SEG = 32
CHUNKS = 1
CAP = 32

water_level = 0.2
epsilon = 1e-05

BF16 = jnp.bfloat16
F32 = jnp.float32


def forward_table(samples):
    bins = np.arange(F, dtype=np.int64) + 1
    times = np.arange(samples, dtype=np.int64)
    angle = 2.0 * np.pi * (bins[:, None] * times[None, :] % samples) / samples
    taper = 0.5 - 0.5 * np.cos(2.0 * np.pi * times / samples)
    return np.concatenate((np.cos(angle) * taper, -np.sin(angle) * taper)).T.astype(np.float32)


def inverse_table(samples):
    bins = np.arange(F, dtype=np.int64) + 1
    shifts = np.arange(LAGS, dtype=np.int64) - LAGS // 2
    angle = 2.0 * np.pi * (bins[:, None] * shifts[None, :] % samples) / samples
    scale = 1.0 / np.sqrt(float(SEG * F))
    return np.concatenate((np.cos(angle) * scale, -np.sin(angle) * scale)).astype(np.float32)


def split_const(table):
    high = table.astype(jnp.bfloat16)
    low = (table - high.astype(np.float32)).astype(jnp.bfloat16)
    return high, low


def split(x):
    high = x.astype(BF16)
    low = (x - high.astype(F32)).astype(BF16)
    return high, low


def dot_nt(a, b):
    return lax.dot_general(a, b, (((1,), (1,)), ((), ())), preferred_element_type=F32)


def dot_nn(a, b):
    return lax.dot_general(a, b, (((1,), (0,)), ((), ())), preferred_element_type=F32)


def whiten_tile(real, imag):
    magnitude = jnp.sqrt(real * real + imag * imag)
    row = lax.broadcasted_iota(jnp.int32, magnitude.shape, 0)
    smoothed = magnitude
    for offset in range(1, SMOOTH + 1):
        smoothed = smoothed + jnp.where(row >= offset, pltpu.roll(magnitude, offset, 0), 0.0)
        smoothed = smoothed + jnp.where(row < F - offset, pltpu.roll(magnitude, F - offset, 0), 0.0)
    water_mark = jnp.mean(magnitude, axis=0, keepdims=True)
    divisor = smoothed * (1.0 / (2 * SMOOTH + 1)) + water_level * water_mark + epsilon
    return real / divisor, imag / divisor


def as_column(row):
    n = row.shape[1]
    here = lax.broadcasted_iota(jnp.int32, (n, n), 0) == lax.broadcasted_iota(jnp.int32, (n, n), 1)
    return jnp.sum(jnp.where(here, row.astype(F32), 0.0), axis=1, keepdims=True).astype(jnp.int32)


def ranks(col, row, channels, axis):
    same = col // channels == row // channels
    first = lax.broadcasted_iota(jnp.int32, same.shape, axis) < lax.broadcasted_iota(jnp.int32, same.shape, 1 - axis)
    return jnp.sum(jnp.where(same & first, 1.0, 0.0), axis=axis, keepdims=True).astype(jnp.int32)


def spectra_kernel(place_ref, rec_ref, hi_ref, lo_ref, row_ref, first_ref, second_ref, held_ref, *, segs):
    step = pl.program_id(0)
    per, channels, samples = rec_ref.shape
    for i in range(per):
        high, low = split(rec_ref[i])
        spectra = dot_nn(high, hi_ref[...]) + (dot_nn(low, hi_ref[...]) + dot_nn(high, lo_ref[...]))
        real, imag = whiten_tile(jnp.transpose(spectra[:, :F]), jnp.transpose(spectra[:, F:]))
        seg = step * per + i
        for ref, start in ((first_ref, 0), (second_ref, first_ref.shape[0] // (2 * segs))):
            count = ref.shape[0] // (2 * segs)
            ref[pl.ds(seg, count, stride=2 * segs), :] = real[start : start + count]
            ref[pl.ds(seg + segs, count, stride=2 * segs), :] = imag[start : start + count]

    @pl.when(step == pl.num_programs(0) - 1)
    def _():
        shards, cap, rows = held_ref.shape
        shard = place_ref[0]
        row = row_ref[...]
        col = as_column(row)
        nsrc = col.shape[0]
        rank = jnp.where(row // channels == shard, ranks(col, row, channels, 0), -1)
        chosen = (lax.broadcasted_iota(jnp.int32, (cap, nsrc), 0) == rank).astype(F32).astype(BF16)
        lane = lax.broadcasted_iota(jnp.int32, (nsrc, channels), 1)
        where = (col - shard * channels == lane).astype(F32).astype(BF16)
        hot = dot_nn(chosen, where).astype(BF16)
        hot = jnp.concatenate((hot, hot), axis=1)
        for d in range(shards):
            cut = first_ref.shape[0] // rows
            ref, at = (first_ref, d) if d < cut else (second_ref, d - cut)
            high, low = split(ref[at * rows : (at + 1) * rows, :])
            held_ref[d] = dot_nt(hot, jnp.concatenate((high, low), axis=1))


def whole(shape):
    return pl.BlockSpec(shape, lambda *_: (0,) * len(shape))


def first_blocks(shards):
    return 5 * shards // 16


def forward(recording, row, shard, shards):
    segs, channels, samples = recording.shape
    per = 4
    nsrc = row.shape[1]
    rows = F // shards * 2 * segs
    held = (shards, CAP, rows)
    cut = first_blocks(shards)
    white = [(cut * rows, channels), ((shards - cut) * rows, channels)]
    high, low = split_const(forward_table(samples))
    return pl.pallas_call(
        functools.partial(spectra_kernel, segs=segs),
        grid_spec=pltpu.PrefetchScalarGridSpec(
            num_scalar_prefetch=1,
            grid=(segs // per,),
            in_specs=[
                pl.BlockSpec((per, channels, samples), lambda s, p: (s, 0, 0)),
                whole((samples, 2 * F)),
                whole((samples, 2 * F)),
                whole((1, nsrc)),
            ],
            out_specs=[whole(x) for x in (*white, held)],
        ),
        out_shape=[jax.ShapeDtypeStruct(x, F32) for x in (*white, held)],
        compiler_params=pltpu.CompilerParams(vmem_limit_bytes=60 * 2**20, dimension_semantics=("arbitrary",)),
        cost_estimate=pl.CostEstimate(flops=6 * 10**9, bytes_accessed=16 * 2**20, transcendentals=0),
        name="forward_whiten",
    )(shard[None], recording, high, low, row)


def order_kernel(place_ref, got_ref, row_ref, *outs, channels):
    row = row_ref[...]
    col = as_column(row)
    nsrc = col.shape[0]
    entries = got_ref.shape[0]
    at = col // channels * CAP + ranks(col, row, channels, 1)
    hot = (at == lax.broadcasted_iota(jnp.int32, (nsrc, entries), 1)).astype(F32).astype(BF16)
    high, low = split(got_ref[...])
    rows = dot_nn(hot, high) + dot_nn(hot, low)
    size = outs[0].shape[0]
    per_half = nsrc // 2
    for h in range(2):

        @pl.when(place_ref[1] == h)
        def _():
            for k, out in enumerate(outs):
                start = ((k // CHUNKS) ^ h) * per_half + k % CHUNKS * size
                out[...] = rows[start : start + size]


def in_order(got, row, shard, half, channels):
    nsrc = row.shape[1]
    size = nsrc // 2 // CHUNKS
    shape = (size, got.shape[1])
    return pl.pallas_call(
        functools.partial(order_kernel, channels=channels),
        grid_spec=pltpu.PrefetchScalarGridSpec(
            num_scalar_prefetch=1,
            grid=(1,),
            in_specs=[whole(got.shape), whole((1, nsrc))],
            out_specs=[whole(shape)] * (2 * CHUNKS),
        ),
        out_shape=[jax.ShapeDtypeStruct(shape, F32)] * (2 * CHUNKS),
        compiler_params=pltpu.CompilerParams(vmem_limit_bytes=16 * 2**20),
        cost_estimate=pl.CostEstimate(flops=10**8, bytes_accessed=2**20, transcendentals=0),
        name="order_sources",
    )(jnp.stack((shard, half)), got, row)


def any_order(white, source_channels, half, shards):
    channels = white.shape[1]
    bins = white.reshape(shards, -1, channels)
    bins = lax.all_to_all(bins, "shard", split_axis=0, concat_axis=2, tiled=True)[0]
    rows = jnp.take(bins, source_channels, axis=1).T
    per_half = rows.shape[0] // 2
    mine = lax.dynamic_slice_in_dim(rows, half * per_half, per_half)
    others = lax.dynamic_slice_in_dim(rows, (1 - half) * per_half, per_half)
    return [*jnp.split(mine, CHUNKS), *jnp.split(others, CHUNKS)]


def stack_kernel(place_ref, own0_ref, own1_ref, oth0_ref, oth1_ref, table_ref, *refs, stacked, pitch):
    stacks = refs[: len(stacked)]
    out_ref, real_ref, imag_ref, src_ref = refs[-4:]
    step = pl.program_id(0)
    per, channels, lags = out_ref.shape
    _, shards, size, lanes = src_ref.shape
    bins = F // shards
    width = lanes // bins
    segs = width // 2
    cut = own0_ref.shape[0] // (bins * width)

    def turn(v):
        return jnp.concatenate((v[segs:], -v[:segs]))

    def block(owner, own_ref, oth_ref, skip):
        for group in range(0, bins, 4):
            lanes = slice(group * width, (group + 4) * width)
            source = [split(src_ref[h, place_ref[0] ^ owner, :, lanes]) for h in range(2)]
            for i in range(group, group + 4):
                rows = pl.ds(pl.multiple_of(((owner - skip) * bins + i) * width, width), width)
                (ah, al), (bh, bl) = split(own_ref[rows, :]), split(oth_ref[rows, :])
                right = (ah, bh, ah, bh, al, bl)
                rhs = jnp.concatenate((jnp.concatenate(right), jnp.concatenate([turn(v) for v in right])), axis=1)
                at = slice((i - group) * width, (i - group + 1) * width)
                (ah, al), (bh, bl) = source
                lhs = jnp.concatenate([v[:, at] for v in (ah, bh, al, bl, ah, bh)], axis=1)
                cross = dot_nn(lhs, rhs)
                to = pl.ds(pl.multiple_of((owner * bins + i) * pitch, 8), size)
                real_ref[to, :] = cross[:, :channels]
                imag_ref[to, :] = cross[:, channels:]

    @pl.when(step == 0)
    def _():
        for held, ref in zip(stacked, stacks):
            for k, (h, r) in enumerate(held):
                src_ref[h, r] = ref[k]

        def four(group, carry, parts):
            for k, (own_ref, oth_ref, skip) in enumerate(parts):
                block(4 * group + k, own_ref, oth_ref, skip)
            return carry

        for group in range(shards // 4):
            parts = [
                (own0_ref, oth0_ref, 0) if owner < cut else (own1_ref, oth1_ref, cut)
                for owner in range(4 * group, 4 * group + 4)
            ]
            lax.fori_loop(group, group + 1, functools.partial(four, parts=parts), 0)

    rows = []
    for i in range(per):
        n = step * per + i
        both = [jnp.transpose(ref[pl.ds(n, F, stride=pitch), :]) for ref in (real_ref, imag_ref)]
        high, low = split(jnp.concatenate(both, axis=1))
        rows.append(jnp.concatenate((high, low, high), axis=1))
    out_ref[...] = dot_nn(jnp.concatenate(rows), table_ref[...]).reshape(per, channels, lags)


def correlate(j, previous, shard, own, other, stacks, samples, sources):
    stacked = [held for held, _ in stacks]
    shards = sum(map(len, stacked)) // 2
    size, lanes = stacks[0][1].shape[1:]
    channels = own[0].shape[1]
    per = 16
    steps = size // per
    pitch = size + 8
    high, low = split_const(inverse_table(samples))
    table = np.concatenate((high, high, low))
    operands = [*own, *other, table, *(x for _, x in stacks)]
    in_specs = [whole(x.shape) for x in operands]
    aliases = {}
    if previous is not None:
        aliases = {1 + len(operands): 0}
        operands.append(previous)
        in_specs.append(pl.BlockSpec(memory_space=pl.ANY))
    return pl.pallas_call(
        functools.partial(stack_kernel, stacked=stacked, pitch=pitch),
        grid_spec=pltpu.PrefetchScalarGridSpec(
            num_scalar_prefetch=1,
            grid=(steps,),
            in_specs=in_specs,
            out_specs=pl.BlockSpec((per, channels, LAGS), lambda s, p: (j * steps + s, 0, 0)),
            scratch_shapes=[
                pltpu.VMEM((F * pitch, channels), F32),
                pltpu.VMEM((F * pitch, channels), F32),
                pltpu.VMEM((2, shards, size, lanes), F32),
            ],
        ),
        out_shape=jax.ShapeDtypeStruct((sources, channels, LAGS), F32),
        input_output_aliases=aliases,
        compiler_params=pltpu.CompilerParams(vmem_limit_bytes=36 * 2**20, dimension_semantics=("arbitrary",)),
        cost_estimate=pl.CostEstimate(flops=20 * 10**9 // CHUNKS, bytes_accessed=48 * 2**20 // CHUNKS, transcendentals=0),
        name="stack_lags",
    )(shard[None], *operands)


def swap(x, axis, bits):
    return lax.ppermute(x, axis, [(i, i ^ bits) for i in range(lax.axis_size(axis))])


def gather(own, crossing, passed):
    crossing, passed = lax.optimization_barrier((crossing, passed))
    other = swap(crossing, "half", 1)
    first = [swap(own, "shard", r) for r in (8, 4, 2)]
    *first, after = lax.optimization_barrier((*first, other))
    second = [swap(after, "shard", r) for r in (8, 4, 2)]
    *two, own, after = lax.optimization_barrier((*first, *second, own, after))
    first, second = two[:3], two[3:]
    mine = jnp.stack((own, after))
    line = jnp.stack((first[0], second[0], first[1], second[1]))
    far = swap(mine, "shard", 12)
    across = swap(line, "shard", 2)
    far, mine, line = lax.optimization_barrier((far, mine, line))
    far_across = swap(far, "shard", 2)
    stacks = []
    for relative, blocks in (
        ((8, 4), line),
        ((0, 2), jnp.concatenate((mine, jnp.stack((first[2], second[2]))))),
        ((10, 6), across),
        ((12, 14), jnp.concatenate((far, far_across))),
    ):
        held = [(h, r) for r in relative for h in range(2)]
        stacks += [(held, blocks), ([(h, r + 1) for h, r in held], swap(blocks, "shard", 1))]
    return stacks, passed, other


def body(recording, source_channels):
    segs, channels, samples = recording.shape
    shards = lax.axis_size("shard")
    shard, half = lax.axis_index("shard"), lax.axis_index("half")
    nsrc = source_channels.shape[0]
    row = source_channels[None, :]
    first, second, held = forward(recording, row, shard, shards)
    other_first = swap(first, "half", 1)

    got = lax.all_to_all(held, "shard", split_axis=0, concat_axis=0, tiled=True)
    mine = in_order(got.reshape(-1, got.shape[2]), row, shard, half, channels)
    counts = jnp.sum(source_channels[:, None] // channels == jnp.arange(shards)[None, :], axis=0)
    mine = lax.cond(
        jnp.max(counts) > CAP,
        lambda m: any_order(jnp.concatenate((first, second)), source_channels, half, shards),
        lambda m: list(m),
        list(mine),
    )
    stacks, other_first, crossed = gather(mine[0], mine[1], other_first)
    second, crossed = lax.optimization_barrier((second, crossed))
    own, other = (first, second), (other_first, swap(second, "half", 1))
    return correlate(0, None, shard, own, other, stacks, samples, nsrc // 2)


def plain_forward_table(samples, freq_count):
    table = forward_table(samples).T
    return jnp.stack((table[:freq_count], table[freq_count:]), axis=1)


def plain_inverse_table(samples, freq_count):
    table = inverse_table(samples)
    return jnp.stack((table[:freq_count], table[freq_count:]), axis=1)


def plain_whiten(spectra):
    magnitude = jnp.sqrt(spectra[:, 0] * spectra[:, 0] + spectra[:, 1] * spectra[:, 1])
    freq_count = magnitude.shape[0]
    padded = jnp.pad(magnitude, ((SMOOTH, SMOOTH), (0, 0), (0, 0)))
    smoothed = padded[0:freq_count]
    for offset in range(1, 2 * SMOOTH + 1):
        smoothed = smoothed + padded[offset : offset + freq_count]
    smoothed = smoothed / (2 * SMOOTH + 1)
    water_mark = jnp.mean(magnitude, axis=0, keepdims=True)
    divisor = smoothed + water_level * water_mark + epsilon
    return spectra / divisor[:, None]


def plain_correlate(whitened, indices):
    sources = jnp.take(whitened, indices, axis=2)
    src_real, src_imag = (sources[:, 0], sources[:, 1])
    rec_real, rec_imag = (whitened[:, 0], whitened[:, 1])
    high = lax.Precision.HIGHEST
    cross_real = jnp.einsum("fnx,fcx->fnc", src_real, rec_real, precision=high) + jnp.einsum(
        "fnx,fcx->fnc", src_imag, rec_imag, precision=high
    )
    cross_imag = jnp.einsum("fnx,fcx->fnc", src_real, rec_imag, precision=high) - jnp.einsum(
        "fnx,fcx->fnc", src_imag, rec_real, precision=high
    )
    return jnp.stack((cross_real, cross_imag), axis=1)


def plain_body(recording, source_channels):
    samples = recording.shape[2]
    high = lax.Precision.HIGHEST
    spectra = jnp.einsum("fqt,sct->fqcs", plain_forward_table(samples, F), recording, precision=high)
    whitened = plain_whiten(spectra)
    by_freq = lax.all_to_all(whitened, "shard", split_axis=0, concat_axis=2, tiled=True)
    per_half = source_channels.shape[0] // lax.axis_size("half")
    own_sources = lax.dynamic_slice_in_dim(source_channels, lax.axis_index("half") * per_half, per_half)
    combined = jnp.concatenate((by_freq, swap(by_freq, "half", 1)), axis=3)
    cross = plain_correlate(combined, own_sources)
    cross = lax.all_to_all(cross, "shard", split_axis=3, concat_axis=0, tiled=True)
    return jnp.einsum("fqnc,fql->ncl", cross, plain_inverse_table(samples, F), precision=high)


def solution(mesh):
    def run(recording, source_channels):
        shards = lax.axis_size("shard")
        fits = recording.shape[1] % 128 == 0 and shards == 16
        return (body if fits else plain_body)(recording, source_channels)

    return jax.shard_map(
        run,
        mesh=mesh,
        in_specs=(P("half", "shard", None), P()),
        out_specs=P("half", "shard", None),
        check_vma=False,
    )
```
